32 devices in a mesh: row: 4 (over y, x), col: 8 (over z, core).
Axes of the slice: x: 2, y: 2, z: 4, core: 2. Of those that a mesh axis runs over, the one named last changes fastest.
Arguments:
- left_site: bfloat16 [4096, 2048], P('row', 'col')
- right_site: bfloat16 [2048, 4096], P('row', 'col'), may hold values from -0.125 to 0.125
- gate: float32 [4, 4], replicated, may hold values from -0.6 to 2.1
- omega: bfloat16 [4096, 2304], P(None, 'row'), may hold values from -0.09375 to 0.09375
Outputs:
- basis: float32 [4096, 2304], P(('row', 'col'))
- projected: float32 [2304, 4096], P('row', 'col')
The draws below stay inside these ranges and needn't reach their ends.
All inputs are finite; a program needn't handle non-finite values.
Results may differ from the reference program's by a relative error of at most 0.0085.
Values may be sent and summed in bfloat16 or wider, within the bound.
No kernel may reach another device: no remote copies, remote signals or barrier semaphores. Data moves between devices by JAX's collectives and lax.ppermute only.
A program may use at most 192 MiB of HBM per device.

```python
import math
import jax
import jax.numpy as jnp
from jax import lax

CHI = 2048
K = 2304
ROWS = 4096


def draw_left_site(key, part):
    noise_key, rough_key = jax.random.split(jax.random.fold_in(key, 11))
    noise = jnp.clip(jax.random.normal(noise_key, (ROWS, CHI), jnp.float32), -4.0, 4.0)
    top_scale = 3.0
    ramp = jnp.arange(ROWS, dtype=jnp.float32) / ROWS
    rough = jnp.exp(jax.random.uniform(rough_key, (ROWS, 1), jnp.float32, -0.35, 0.35))
    scales = jnp.power(top_scale, ramp)[:, None] * rough
    return (noise * scales).astype(jnp.bfloat16)


def draw_gate(key, part):
    entries = jax.random.uniform(jax.random.fold_in(key, 23), (4, 4), jnp.float32, -0.6, 0.6)
    return entries + 1.5 * jnp.eye(4, dtype=jnp.float32)


def steps_of(own_key, dims, cuts, low, high):
    loudness = 1.0
    for axis_at, parts in cuts:
        draws = jax.random.uniform(jax.random.fold_in(jax.random.fold_in(own_key, 6), axis_at), (parts,), jnp.float32, low / len(cuts), high / len(cuts))
        loudness = loudness * jnp.repeat(jnp.exp(draws), dims[axis_at] // parts).reshape((-1,) + (1,) * (len(dims) - 1 - axis_at))
    return loudness


def centred(own_key, extent, scale, bound, pieces=(), kind=jnp.bfloat16):
    loudness = steps_of(own_key, extent, pieces, -0.22, 0.18) if pieces else 1.0
    drawn = jax.random.normal(own_key, extent, jnp.float32) * scale * loudness
    return jnp.minimum(jnp.maximum(drawn, -bound), bound).astype(kind)


def setup_inputs(seed: int = 0) -> dict:
    keys = jax.random.split(jax.random.key(seed), 5)
    return {
        "left_site": draw_left_site(jax.random.fold_in(keys[4], 71), 0),
        "right_site": centred(keys[1], (CHI, ROWS), CHI ** -0.5, 0.125, ((0, 4), (1, 8))),
        "gate": draw_gate(jax.random.fold_in(keys[4], 71), 0),
        "omega": centred(keys[3], (ROWS, K), ROWS ** -0.5, 0.09375, ((1, 4),)),
    }


def reference(left_site, right_site, gate, omega):
    bare = jnp.dot(left_site.astype(jnp.float32), right_site.astype(jnp.float32), preferred_element_type=jnp.float32)
    quad = bare.reshape(CHI, 2, CHI, 2)
    gate_four = gate.astype(jnp.float32).reshape(2, 2, 2, 2)
    mixed = jnp.einsum('pqab,larb->lprq', gate_four, quad, precision=lax.Precision.HIGHEST)
    theta = mixed.reshape(ROWS, ROWS).astype(jnp.bfloat16)
    sketch = jnp.dot(theta.astype(jnp.float32), omega.astype(jnp.float32), preferred_element_type=jnp.float32)
    gram = jnp.dot(sketch.T, sketch, precision=lax.Precision.HIGHEST) / ROWS
    factor = jnp.linalg.cholesky(gram)
    basis = jax.scipy.linalg.solve_triangular(factor, sketch.T, lower=True).T
    projected = jnp.dot(basis.T, theta.astype(jnp.float32), precision=lax.Precision.HIGHEST) / math.sqrt(ROWS)
    return (basis, projected)
```

```python
import functools
import math

import jax
import jax.numpy as jnp
from jax import lax
from jax.experimental import pallas as pl
from jax.experimental.pallas import tpu as pltpu
from jax.sharding import PartitionSpec as P

F32, BF16 = jnp.float32, jnp.bfloat16
NN = (((1,), (0,)), ((), ()))
NT = (((1,), (1,)), ((), ()))
TN = (((0,), (0,)), ((), ()))
VMEM = pl.BlockSpec(memory_space=pltpu.VMEM)
TILE = 256
ROUGH_STEPS = 5
SETTLED = 1e-4


def dot(a, b, dims=NN):
    return lax.dot_general(a, b, dims, preferred_element_type=F32)


def halves(x):
    high = x.astype(BF16)
    return high, (x - high.astype(F32)).astype(BF16)


def dot3(a, b, dims=NN):
    return dot(a[0], b[0], dims) + dot(a[0], b[1], dims) + dot(a[1], b[0], dims)


def positions(shape):
    return lax.broadcasted_iota(jnp.int32, shape, 0), lax.broadcasted_iota(jnp.int32, shape, 1)


def theta_kernel(gate_ref, left_ref, right_ref, theta_ref):
    bare = dot(left_ref[...], right_ref[...])
    rows, cols = bare.shape
    row, col = positions((rows, cols))
    row_odd, col_odd = row % 2 == 1, col % 2 == 1

    def partner_row(x):
        return jnp.where(row_odd, pltpu.roll(x, 1, 0), pltpu.roll(x, rows - 1, 0))

    def partner_col(x):
        return jnp.where(col_odd, pltpu.roll(x, 1, 1), pltpu.roll(x, cols - 1, 1))

    def weight(flip_row, flip_col):
        def entry(s, t):
            return gate_ref[2 * s + t, 2 * (s ^ flip_row) + (t ^ flip_col)]

        return jnp.where(
            row_odd,
            jnp.where(col_odd, entry(1, 1), entry(1, 0)),
            jnp.where(col_odd, entry(0, 1), entry(0, 0)),
        )

    across = partner_row(bare)
    mixed = weight(0, 0) * bare + weight(0, 1) * partner_col(bare)
    mixed = mixed + weight(1, 0) * across + weight(1, 1) * partner_col(across)
    theta_ref[...] = mixed.astype(BF16)


def theta_of(left, right, gate):
    rows, depth = left.shape
    cols = right.shape[1]
    return pl.pallas_call(
        theta_kernel,
        grid=(rows // TILE,),
        out_shape=jax.ShapeDtypeStruct((rows, cols), BF16),
        in_specs=[
            pl.BlockSpec(memory_space=pltpu.SMEM),
            pl.BlockSpec((TILE, depth), lambda i: (i, 0)),
            pl.BlockSpec((depth, cols), lambda i: (0, 0)),
        ],
        out_specs=pl.BlockSpec((TILE, cols), lambda i: (i, 0)),
        compiler_params=pltpu.CompilerParams(vmem_limit_bytes=32 << 20),
        cost_estimate=pl.CostEstimate(
            flops=2 * rows * depth * cols,
            bytes_accessed=2 * (rows * depth + depth * cols + rows * cols),
            transcendentals=0,
        ),
    )(gate, left, right)


def eliminate(block, out_ref, work_ref):
    tile = block.shape[0]
    row, col = positions((tile, tile))
    work_ref[...] = block
    out_ref[...] = jnp.where(row == col, 1.0, 0.0).astype(F32)

    def column(j, carry):
        values = work_ref[...]
        pivot_row = work_ref[pl.ds(j, 1), :]
        pivot_col = jnp.sum(jnp.where(col == j, values, 0.0), axis=1, keepdims=True)
        pivot = jnp.sum(jnp.where(col[:1] == j, pivot_row, 0.0), axis=1, keepdims=True)
        root = 1.0 / jnp.sqrt(pivot)
        done = out_ref[pl.ds(j, 1), :] * root
        factor = jnp.where(row[:, :1] > j, pivot_col * root, 0.0)
        work_ref[...] = values - factor * (pivot_row * root)
        out_ref[...] = out_ref[...] - factor * done
        out_ref[pl.ds(j, 1), :] = done
        return carry

    lax.fori_loop(0, tile, column, 0)


def inverse_factor(block, out_ref, work_ref):
    row, col = positions(block.shape)
    same, below = row == col, row > col
    diagonal = jnp.where(same, block, 0.0)
    scale_row = lax.rsqrt(jnp.sum(diagonal, axis=0, keepdims=True))
    scale_col = lax.rsqrt(jnp.sum(diagonal, axis=1, keepdims=True))
    normal = block * scale_row * scale_col
    parts = halves(normal)
    near = 0.5 * normal
    inverse = jnp.where(same, math.sqrt(0.5), 0.0).astype(F32)
    for _ in range(ROUGH_STEPS):
        step = jnp.where(below, -near, jnp.where(same, 1.5 - 0.5 * near, 0.0)).astype(BF16)
        inverse = dot(step, inverse.astype(BF16))
        near = dot(dot(step, near.astype(BF16)).astype(BF16), step, NT)

    def polish(inverse):
        own = halves(inverse)
        rest = dot3(halves(dot3(own, parts)), own, NT) - jnp.where(same, 1.0, 0.0)
        shift = jnp.where(below, rest, jnp.where(same, 0.5 * rest, 0.0)).astype(BF16)
        return inverse - dot(shift, own[0]), jnp.sum(rest * rest)

    inverse, _ = polish(inverse)
    inverse, gap = polish(inverse)
    out_ref[...] = inverse

    def again(state):
        inverse, gap = polish(out_ref[...])
        out_ref[...] = inverse
        return state[0] + 1, gap

    _, gap = lax.while_loop(lambda state: (state[0] < 16) & (state[1] > SETTLED), again, (0, gap))
    settled = gap <= SETTLED

    @pl.when(settled)
    def _():
        out_ref[...] = out_ref[...] * scale_row

    @pl.when(jnp.logical_not(settled))
    def _():
        eliminate(block, out_ref, work_ref)


def basis_kernel(scale, *refs):
    count = len(refs) - 10
    gram_refs, sketch_ref = refs[:count], refs[count]
    basis_ref, short_ref, high_ref, low_ref, basis_low_ref, inv_high_ref, inv_low_ref, inverse_ref, work_ref = refs[
        count + 1 :
    ]
    for k in range(count):
        here, past = slice(k * TILE, (k + 1) * TILE), slice(0, k * TILE)
        gram_ref = gram_refs[k]

        def left_over(values, left):
            if k == 0:
                return values
            return values - dot3(left, (high_ref[here, past], low_ref[here, past]), NT)

        def factor_rows(at):
            return high_ref[pl.ds(at, TILE), past], low_ref[pl.ds(at, TILE), past]

        inverse_factor(
            left_over(gram_ref[:TILE, :] * scale, factor_rows(k * TILE) if k else None), inverse_ref, work_ref
        )
        inv_high_ref[...], inv_low_ref[...] = halves(inverse_ref[...])

        def panel(i, carry):
            own = inv_high_ref[...], inv_low_ref[...]
            at = pl.multiple_of((k + 1 + i) * TILE, TILE)
            gram_at = pl.multiple_of((1 + i) * TILE, TILE)
            values = left_over(gram_ref[pl.ds(gram_at, TILE), :] * scale, factor_rows(at) if k else None)
            solved = halves(dot3(halves(values), own, NT))
            high_ref[pl.ds(at, TILE), here], low_ref[pl.ds(at, TILE), here] = solved
            return carry

        if k + 1 < count:
            lax.fori_loop(0, count - 1 - k, panel, 0)
        values = left_over(sketch_ref[:, here], (short_ref[:, past], basis_low_ref[:, past]) if k else None)
        solved = dot3(halves(values), (inv_high_ref[...], inv_low_ref[...]), NT)
        basis_ref[:, here] = solved
        short_ref[:, here], basis_low_ref[:, here] = halves(solved)


def basis_of(gram_columns, sketch, scale):
    rows, size = sketch.shape
    return pl.pallas_call(
        functools.partial(basis_kernel, scale),
        out_shape=[jax.ShapeDtypeStruct((rows, size), F32), jax.ShapeDtypeStruct((rows, size), BF16)],
        in_specs=[VMEM] * (len(gram_columns) + 1),
        out_specs=[VMEM, VMEM],
        scratch_shapes=[
            pltpu.VMEM((size, size), BF16),
            pltpu.VMEM((size, size), BF16),
            pltpu.VMEM((rows, size), BF16),
            pltpu.VMEM((TILE, TILE), BF16),
            pltpu.VMEM((TILE, TILE), BF16),
            pltpu.VMEM((TILE, TILE), F32),
            pltpu.VMEM((TILE, TILE), F32),
        ],
        compiler_params=pltpu.CompilerParams(vmem_limit_bytes=56 << 20),
        cost_estimate=pl.CostEstimate(
            flops=24 * size**3, bytes_accessed=2 * size * size + 10 * rows * size, transcendentals=0
        ),
    )(*gram_columns, sketch)


def gram_columns_of(sketch):
    rounded = lax.reduce_precision(sketch, 8, 7)
    high, low = rounded.astype(BF16), (sketch - rounded).astype(BF16)
    left = jnp.concatenate([high, high, low], axis=0)
    right = jnp.concatenate([high, low, high], axis=0)
    return tuple(
        dot(left[:, at:], right[:, at : at + TILE], TN) for at in range(0, sketch.shape[1], TILE)
    )


def on_device(left_site, right_site, gate, omega):
    rows_here = left_site.shape[0]
    total_rows = rows_here * lax.axis_size("row")
    right_cols = lax.all_gather(right_site, "row", axis=0, tiled=True)
    left_rows = lax.all_gather(left_site, "col", axis=1, tiled=True)
    theta = theta_of(left_rows, right_cols, gate)
    cols_here = theta.shape[1]
    omega_mine = lax.dynamic_slice_in_dim(omega, lax.axis_index("col") * cols_here, cols_here, 0)
    omega_rows = lax.all_gather(omega_mine, "row", axis=1, tiled=True)
    sketch = lax.psum_scatter(dot(theta, omega_rows), "col", scatter_dimension=0, tiled=True)
    gram_columns = lax.psum(gram_columns_of(sketch), ("row", "col"))
    basis, basis_short = basis_of(gram_columns, sketch, 1.0 / total_rows)
    basis_rows = lax.all_gather(basis_short, "col", axis=0, tiled=True)
    folded = dot(basis_rows, theta, TN).astype(BF16)
    pieces = lax.all_to_all(
        folded.reshape(lax.axis_size("row"), -1, cols_here), "row", 0, 0, tiled=False
    )
    projected = jnp.sum(pieces.astype(F32), axis=0) / math.sqrt(total_rows)
    return (basis, projected)


def solution(mesh):
    in_specs = (P("row", "col"), P("row", "col"), P(), P(None, "row"))
    out_specs = (P(("row", "col"), None), P("row", "col"))
    return jax.shard_map(
        on_device, mesh=mesh, in_specs=in_specs, out_specs=out_specs, check_vma=False
    )
```

```python
import functools
import math

import jax
import jax.numpy as jnp
from jax import lax
from jax.experimental import pallas as pl
from jax.experimental.pallas import tpu as pltpu
from jax.sharding import Mesh, PartitionSpec as P

F32, BF16 = jnp.float32, jnp.bfloat16
NN = (((1,), (0,)), ((), ()))
NT = (((1,), (1,)), ((), ()))
TN = (((0,), (0,)), ((), ()))
VMEM = pl.BlockSpec(memory_space=pltpu.VMEM)
SMEM = pl.BlockSpec(memory_space=pltpu.SMEM)
ANY = pl.BlockSpec(memory_space=pl.ANY)
TILE = 256
ROUGH_STEPS = 5
SETTLED = 1e-4


def dot(a, b, dims=NN):
    return lax.dot_general(a, b, dims, preferred_element_type=F32)


def halves(x):
    high = x.astype(BF16)
    return high, (x - high.astype(F32)).astype(BF16)


def dot3(a, b, dims=NN):
    return dot(a[0], b[0], dims) + dot(a[0], b[1], dims) + dot(a[1], b[0], dims)


def positions(shape):
    return lax.broadcasted_iota(jnp.int32, shape, 0), lax.broadcasted_iota(jnp.int32, shape, 1)


def theta_kernel(gate_ref, left_ref, right_ref, theta_ref):
    bare = dot(left_ref[...], right_ref[...])
    rows, cols = bare.shape
    row, col = positions((rows, cols))
    row_odd, col_odd = row % 2 == 1, col % 2 == 1

    def partner_row(x):
        return jnp.where(row_odd, pltpu.roll(x, 1, 0), pltpu.roll(x, rows - 1, 0))

    def partner_col(x):
        return jnp.where(col_odd, pltpu.roll(x, 1, 1), pltpu.roll(x, cols - 1, 1))

    def weight(flip_row, flip_col):
        def entry(s, t):
            return gate_ref[2 * s + t, 2 * (s ^ flip_row) + (t ^ flip_col)]

        return jnp.where(
            row_odd,
            jnp.where(col_odd, entry(1, 1), entry(1, 0)),
            jnp.where(col_odd, entry(0, 1), entry(0, 0)),
        )

    across = partner_row(bare)
    mixed = weight(0, 0) * bare + weight(0, 1) * partner_col(bare)
    mixed = mixed + weight(1, 0) * across + weight(1, 1) * partner_col(across)
    theta_ref[...] = mixed.astype(BF16)


def theta_of(left, right, gate):
    rows, depth = left.shape
    cols = right.shape[1]
    return pl.pallas_call(
        theta_kernel,
        grid=(rows // TILE,),
        out_shape=jax.ShapeDtypeStruct((rows, cols), BF16),
        in_specs=[
            pl.BlockSpec(memory_space=pltpu.SMEM),
            pl.BlockSpec((TILE, depth), lambda i: (i, 0)),
            pl.BlockSpec((depth, cols), lambda i: (0, 0)),
        ],
        out_specs=pl.BlockSpec((TILE, cols), lambda i: (i, 0)),
        compiler_params=pltpu.CompilerParams(vmem_limit_bytes=32 << 20),
        cost_estimate=pl.CostEstimate(
            flops=2 * rows * depth * cols,
            bytes_accessed=2 * (rows * depth + depth * cols + rows * cols),
            transcendentals=0,
        ),
    )(gate, left, right)


def eliminate(block, out_ref, work_ref):
    tile = block.shape[0]
    row, col = positions((tile, tile))
    work_ref[...] = block
    out_ref[...] = jnp.where(row == col, 1.0, 0.0).astype(F32)

    def column(j, carry):
        values = work_ref[...]
        pivot_row = work_ref[pl.ds(j, 1), :]
        pivot_col = jnp.sum(jnp.where(col == j, values, 0.0), axis=1, keepdims=True)
        pivot = jnp.sum(jnp.where(col[:1] == j, pivot_row, 0.0), axis=1, keepdims=True)
        root = 1.0 / jnp.sqrt(pivot)
        done = out_ref[pl.ds(j, 1), :] * root
        factor = jnp.where(row[:, :1] > j, pivot_col * root, 0.0)
        work_ref[...] = values - factor * (pivot_row * root)
        out_ref[...] = out_ref[...] - factor * done
        out_ref[pl.ds(j, 1), :] = done
        return carry

    lax.fori_loop(0, tile, column, 0)


def inverse_factor(block, out_ref, work_ref):
    row, col = positions(block.shape)
    same, below = row == col, row > col
    diagonal = jnp.where(same, block, 0.0)
    scale_row = lax.rsqrt(jnp.sum(diagonal, axis=0, keepdims=True))
    scale_col = lax.rsqrt(jnp.sum(diagonal, axis=1, keepdims=True))
    normal = block * scale_row * scale_col
    parts = halves(normal)
    near = 0.5 * normal
    inverse = jnp.where(same, math.sqrt(0.5), 0.0).astype(F32)
    for _ in range(ROUGH_STEPS):
        step = jnp.where(below, -near, jnp.where(same, 1.5 - 0.5 * near, 0.0)).astype(BF16)
        inverse = dot(step, inverse.astype(BF16))
        near = dot(dot(step, near.astype(BF16)).astype(BF16), step, NT)

    def polish(inverse):
        own = halves(inverse)
        rest = dot3(halves(dot3(own, parts)), own, NT) - jnp.where(same, 1.0, 0.0)
        shift = jnp.where(below, rest, jnp.where(same, 0.5 * rest, 0.0)).astype(BF16)
        return inverse - dot(shift, own[0]), jnp.sum(rest * rest)

    inverse, _ = polish(inverse)
    inverse, gap = polish(inverse)
    out_ref[...] = inverse

    def again(state):
        inverse, gap = polish(out_ref[...])
        out_ref[...] = inverse
        return state[0] + 1, gap

    _, gap = lax.while_loop(lambda state: (state[0] < 16) & (state[1] > SETTLED), again, (0, gap))
    settled = gap <= SETTLED

    @pl.when(settled)
    def _():
        out_ref[...] = out_ref[...] * scale_row

    @pl.when(jnp.logical_not(settled))
    def _():
        eliminate(block, out_ref, work_ref)


def tiles_before(k, count):
    return k * count - k * (k - 1) // 2


def shared_tiles(count):
    total = count * (count + 1) // 2
    return total + total % 2


def gram_kernel(parts, spot_ref, *refs):
    piece_refs, gram_ref = refs[:parts], refs[parts]
    sketch_ref, high_ref, low_ref, own_high_ref, own_low_ref, sems = refs[parts + 1 :]
    spot = spot_ref[0]
    size = sketch_ref.shape[0]
    width, part = size // parts, TILE // parts
    count = size // TILE
    copies = [
        pltpu.make_async_copy(
            piece_refs[d], sketch_ref.at[pl.ds(pl.multiple_of((spot ^ d) * width, 16), width), :], sems.at[d]
        )
        for d in range(parts)
    ]
    for copy in copies:
        copy.start()
    for copy in copies:
        copy.wait()
    for i in range(count):
        here = slice(i * TILE, (i + 1) * TILE)
        high_ref[here, :], low_ref[here, :] = halves(sketch_ref[here, :])
    for i in range(count):
        at = pl.multiple_of(i * TILE + spot * part, 16)
        own_high_ref[i * part : (i + 1) * part, :] = high_ref[pl.ds(at, part), :]
        own_low_ref[i * part : (i + 1) * part, :] = low_ref[pl.ds(at, part), :]
    for k in range(count):
        here = slice(k * TILE, (k + 1) * TILE)
        start = tiles_before(k, count) * part
        gram_ref[start : start + (count - k) * part, :] = dot3(
            (own_high_ref[k * part :, :], own_low_ref[k * part :, :]), (high_ref[here, :], low_ref[here, :]), NT
        )
    total = tiles_before(count, count) * part
    if total < gram_ref.shape[0]:
        gram_ref[total:, :] = jnp.zeros((gram_ref.shape[0] - total, TILE), F32)


def gram_share(spot, pieces):
    parts = len(pieces)
    width, rows = pieces[0].shape
    size = parts * width
    count, part = size // TILE, TILE // parts
    return pl.pallas_call(
        functools.partial(gram_kernel, parts),
        out_shape=jax.ShapeDtypeStruct((shared_tiles(count) * part, TILE), F32),
        in_specs=[SMEM] + [ANY] * parts,
        out_specs=VMEM,
        scratch_shapes=[
            pltpu.VMEM((size, rows), F32),
            pltpu.VMEM((size, rows), BF16),
            pltpu.VMEM((size, rows), BF16),
            pltpu.VMEM((count * part, rows), BF16),
            pltpu.VMEM((count * part, rows), BF16),
            pltpu.SemaphoreType.DMA((parts,)),
        ],
        compiler_params=pltpu.CompilerParams(vmem_limit_bytes=40 << 20),
        cost_estimate=pl.CostEstimate(
            flops=3 * size * size * rows // parts, bytes_accessed=8 * size * rows, transcendentals=0
        ),
    )(spot, *pieces)


def basis_kernel(scale, parts, spot_ref, *refs):
    shares = refs[: 2 * parts]
    sketch_ref, basis_ref, short_ref, gram_ref, high_ref, low_ref, basis_low_ref, inv_high_ref, inv_low_ref = refs[
        2 * parts : 2 * parts + 9
    ]
    inverse_ref, work_ref, sems = refs[2 * parts + 9 :]
    size = high_ref.shape[0]
    count, part = size // TILE, TILE // parts
    half = gram_ref.shape[2] // part
    spot, core = spot_ref[0], spot_ref[1]
    copies = [
        pltpu.make_async_copy(shares[e * parts + d], gram_ref.at[core ^ e, spot ^ d], sems.at[e * parts + d])
        for e in range(2)
        for d in range(parts)
    ]
    for copy in copies:
        copy.start()
    for copy in copies:
        copy.wait()

    def gram_tile(index):
        if isinstance(index, int):
            owner, at = index // half, index % half * part
        else:
            owner = (index >= half).astype(jnp.int32)
            at = pl.multiple_of((index - owner * half) * part, part)
        return scale * jnp.concatenate(
            [gram_ref[owner, sub, pl.ds(at, part), :] for sub in range(parts)], axis=0
        )

    for k in range(count):
        here, past = slice(k * TILE, (k + 1) * TILE), slice(0, k * TILE)
        first = tiles_before(k, count)

        def left_over(values, left):
            if k == 0:
                return values
            return values - dot3(left, (high_ref[here, past], low_ref[here, past]), NT)

        def factor_rows(at):
            return (high_ref[pl.ds(at, TILE), past], low_ref[pl.ds(at, TILE), past]) if k else None

        inverse_factor(left_over(gram_tile(first), factor_rows(k * TILE)), inverse_ref, work_ref)
        inv_high_ref[...], inv_low_ref[...] = halves(inverse_ref[...])

        def panel(i, carry):
            own = inv_high_ref[...], inv_low_ref[...]
            at = pl.multiple_of((k + 1 + i) * TILE, TILE)
            values = left_over(gram_tile(first + 1 + i), factor_rows(at))
            solved = halves(dot3(halves(values), own, NT))
            high_ref[pl.ds(at, TILE), here], low_ref[pl.ds(at, TILE), here] = solved
            return carry

        if k + 1 < count:
            lax.fori_loop(0, count - 1 - k, panel, 0)
        values = left_over(sketch_ref[:, here], (short_ref[:, past], basis_low_ref[:, past]) if k else None)
        solved = dot3(halves(values), (inv_high_ref[...], inv_low_ref[...]), NT)
        basis_ref[:, here] = solved
        short_ref[:, here], basis_low_ref[:, here] = halves(solved)


def basis_of(spots, shares, sketch, scale):
    rows, size = sketch.shape
    parts = len(shares) // 2
    return pl.pallas_call(
        functools.partial(basis_kernel, scale, parts),
        out_shape=[jax.ShapeDtypeStruct((rows, size), F32), jax.ShapeDtypeStruct((rows, size), BF16)],
        in_specs=[SMEM] + [ANY] * (2 * parts) + [VMEM],
        out_specs=[VMEM, VMEM],
        scratch_shapes=[
            pltpu.VMEM((2, parts) + shares[0].shape, F32),
            pltpu.VMEM((size, size), BF16),
            pltpu.VMEM((size, size), BF16),
            pltpu.VMEM((rows, size), BF16),
            pltpu.VMEM((TILE, TILE), BF16),
            pltpu.VMEM((TILE, TILE), BF16),
            pltpu.VMEM((TILE, TILE), F32),
            pltpu.VMEM((TILE, TILE), F32),
            pltpu.SemaphoreType.DMA((2 * parts,)),
        ],
        compiler_params=pltpu.CompilerParams(vmem_limit_bytes=56 << 20),
        cost_estimate=pl.CostEstimate(
            flops=24 * size**3, bytes_accessed=2 * size * size + 10 * rows * size, transcendentals=0
        ),
    )(spots, *shares, sketch)


def swapped(x, axis, distance):
    return lax.ppermute(x, axis, [(i, i ^ distance) for i in range(lax.axis_size(axis))])


def together(*arrays):
    return lax.optimization_barrier(arrays)


def row_pieces(x):
    size = lax.axis_size("row")
    if size != 4:
        return [x] + [swapped(x, "row", d) for d in range(1, size)]
    half = x.shape[0] // 2
    first, second = x[:half], x[half:]
    first_one, second_two, first_two, second_one = together(
        swapped(first, "row", 1), swapped(second, "row", 2), swapped(first, "row", 2), swapped(second, "row", 1)
    )
    first_three, second_three = together(swapped(first_one, "row", 2), swapped(second_two, "row", 1))
    return [
        x,
        jnp.concatenate([first_one, second_one]),
        jnp.concatenate([first_two, second_two]),
        jnp.concatenate([first_three, second_three]),
    ]


def in_row_order(pieces, axis, place):
    shape = list(pieces[0].shape)
    step = shape[axis]
    shape[axis] *= len(pieces)
    whole = jnp.zeros(shape, pieces[0].dtype)
    for d, piece in enumerate(pieces):
        whole = lax.dynamic_update_slice_in_dim(whole, piece, (place ^ d) * step, axis)
    return whole


def on_device(left_site, right_site, gate, omega):
    rows_here = left_site.shape[0]
    total_rows = rows_here * lax.axis_size("row")
    place, core = lax.axis_index("row"), lax.axis_index("core")
    spot = place.astype(jnp.int32).reshape(1)
    left_rows = lax.all_gather(left_site, COL, axis=1, tiled=True)
    right_cols = in_row_order(row_pieces(right_site), 0, place)
    theta = theta_of(left_rows, right_cols, gate)
    cols_here = theta.shape[1]

    theta_rows = lax.all_to_all(theta, COL, 0, 1, tiled=True)
    rows = theta_rows.shape[0]
    theta_set = in_row_order(row_pieces(theta_rows), 0, place)
    sketch_share = dot(omega, theta_set, (((0,), (1,)), ((), ())))
    pieces = row_pieces(sketch_share)
    sketch = in_row_order(
        [lax.dynamic_slice_in_dim(piece, place * rows, rows, 1).T for piece in pieces], 1, place
    )

    share = gram_share(spot, pieces)
    half = share.shape[0] // 2
    kept = lax.dynamic_slice_in_dim(share, core * half, half, 0)
    given = lax.dynamic_slice_in_dim(share, (1 - core) * half, half, 0)
    kept = kept + swapped(given, "core", 1)
    chips = lax.axis_size("chip")
    kept = jnp.sum(lax.all_to_all(kept.reshape(chips, half // chips, TILE), "chip", 0, 0), axis=0)
    mine = row_pieces(lax.all_gather(kept, "chip", axis=0, tiled=True))
    others = [swapped(piece, "core", 1) for piece in mine]
    spots = jnp.stack([place, core]).astype(jnp.int32)
    basis, basis_short = basis_of(spots, mine + others, sketch, 1.0 / total_rows)

    basis_rows = lax.all_gather(basis_short, COL, axis=0, tiled=True)
    folded = dot(basis_rows, theta, TN).astype(BF16)
    folded = folded.reshape(lax.axis_size("row"), -1, cols_here)
    sums = lax.all_to_all(folded, "row", 0, 0)
    projected = jnp.sum(sums.astype(F32), axis=0) / math.sqrt(total_rows)
    return (basis, projected)


COL = ("chip", "core")


def solution(mesh):
    row, col = mesh.devices.shape
    split = Mesh(mesh.devices.reshape(row, col // 2, 2), ("row",) + COL)
    in_specs = (P("row", COL), P("row", COL), P(), P(None, "row"))
    out_specs = (P(("row",) + COL, None), P("row", COL))
    return jax.shard_map(
        on_device, mesh=split, in_specs=in_specs, out_specs=out_specs, check_vma=False
    )
```

```python
import functools
import math

import jax
import jax.numpy as jnp
from jax import lax
from jax.experimental import pallas as pl
from jax.experimental.pallas import tpu as pltpu
from jax.sharding import Mesh, PartitionSpec as P

F32, BF16 = jnp.float32, jnp.bfloat16
NN = (((1,), (0,)), ((), ()))
NT = (((1,), (1,)), ((), ()))
TN = (((0,), (0,)), ((), ()))
VMEM = pl.BlockSpec(memory_space=pltpu.VMEM)
SMEM = pl.BlockSpec(memory_space=pltpu.SMEM)
ANY = pl.BlockSpec(memory_space=pl.ANY)
TILE = 256
ROUGH_STEPS = 5
SETTLED = 1e-4


def dot(a, b, dims=NN):
    return lax.dot_general(a, b, dims, preferred_element_type=F32)


def halves(x):
    high = x.astype(BF16)
    return high, (x - high.astype(F32)).astype(BF16)


def dot3(a, b, dims=NN):
    return dot(a[0], b[0], dims) + dot(a[0], b[1], dims) + dot(a[1], b[0], dims)


def positions(shape):
    return lax.broadcasted_iota(jnp.int32, shape, 0), lax.broadcasted_iota(jnp.int32, shape, 1)


def theta_kernel(chips, gate_ref, spot_ref, *refs):
    left_refs, right_ref, theta_ref = refs[:-2], refs[-2], refs[-1]
    depth = left_refs[0].shape[1]
    bare = None
    for n, left_ref in enumerate(left_refs):
        e, d = divmod(n, chips)
        at = ((spot_ref[2] ^ d) * 2 + (spot_ref[1] ^ e)) * depth
        product = dot(left_ref[...], right_ref[pl.ds(pl.multiple_of(at, depth), depth), :])
        bare = product if bare is None else bare + product
    rows, cols = bare.shape
    row, col = positions((rows, cols))
    row_odd, col_odd = row % 2 == 1, col % 2 == 1

    def partner_row(x):
        return jnp.where(row_odd, pltpu.roll(x, 1, 0), pltpu.roll(x, rows - 1, 0))

    def partner_col(x):
        return jnp.where(col_odd, pltpu.roll(x, 1, 1), pltpu.roll(x, cols - 1, 1))

    def weight(flip_row, flip_col):
        def entry(s, t):
            return gate_ref[2 * s + t, 2 * (s ^ flip_row) + (t ^ flip_col)]

        return jnp.where(
            row_odd,
            jnp.where(col_odd, entry(1, 1), entry(1, 0)),
            jnp.where(col_odd, entry(0, 1), entry(0, 0)),
        )

    across = partner_row(bare)
    mixed = weight(0, 0) * bare + weight(0, 1) * partner_col(bare)
    mixed = mixed + weight(1, 0) * across + weight(1, 1) * partner_col(across)
    theta_ref[...] = mixed.astype(BF16)


def theta_of(gate, spots, pieces, right):
    rows, depth = pieces[0].shape
    cols = right.shape[1]
    tile = min(TILE, rows)
    return pl.pallas_call(
        functools.partial(theta_kernel, len(pieces) // 2),
        grid=(rows // tile,),
        out_shape=jax.ShapeDtypeStruct((rows, cols), BF16),
        in_specs=[SMEM, SMEM]
        + [pl.BlockSpec((tile, depth), lambda i: (i, 0))] * len(pieces)
        + [pl.BlockSpec(right.shape, lambda i: (0, 0))],
        out_specs=pl.BlockSpec((tile, cols), lambda i: (i, 0)),
        compiler_params=pltpu.CompilerParams(vmem_limit_bytes=32 << 20),
        cost_estimate=pl.CostEstimate(
            flops=rows * cols,
            bytes_accessed=rows * cols,
            transcendentals=0,
        ),
    )(gate, spots, *pieces, right)


def eliminate(block, out_ref, work_ref):
    tile = block.shape[0]
    row, col = positions((tile, tile))
    work_ref[...] = block
    out_ref[...] = jnp.where(row == col, 1.0, 0.0).astype(F32)

    def column(j, carry):
        values = work_ref[...]
        pivot_row = work_ref[pl.ds(j, 1), :]
        pivot_col = jnp.sum(jnp.where(col == j, values, 0.0), axis=1, keepdims=True)
        pivot = jnp.sum(jnp.where(col[:1] == j, pivot_row, 0.0), axis=1, keepdims=True)
        root = 1.0 / jnp.sqrt(pivot)
        done = out_ref[pl.ds(j, 1), :] * root
        factor = jnp.where(row[:, :1] > j, pivot_col * root, 0.0)
        work_ref[...] = values - factor * (pivot_row * root)
        out_ref[...] = out_ref[...] - factor * done
        out_ref[pl.ds(j, 1), :] = done
        return carry

    lax.fori_loop(0, tile, column, 0)


def inverse_factor(block, out_ref, work_ref):
    row, col = positions(block.shape)
    same, below = row == col, row > col
    diagonal = jnp.where(same, block, 0.0)
    scale_row = lax.rsqrt(jnp.sum(diagonal, axis=0, keepdims=True))
    scale_col = lax.rsqrt(jnp.sum(diagonal, axis=1, keepdims=True))
    normal = block * scale_row * scale_col
    parts = halves(normal)
    near = 0.5 * normal
    inverse = jnp.where(same, math.sqrt(0.5), 0.0).astype(F32)
    for _ in range(ROUGH_STEPS):
        step = jnp.where(below, -near, jnp.where(same, 1.5 - 0.5 * near, 0.0)).astype(BF16)
        inverse = dot(step, inverse.astype(BF16))
        near = dot(dot(step, near.astype(BF16)).astype(BF16), step, NT)

    def polish(inverse):
        own = halves(inverse)
        rest = dot3(halves(dot3(own, parts)), own, NT) - jnp.where(same, 1.0, 0.0)
        shift = jnp.where(below, rest, jnp.where(same, 0.5 * rest, 0.0)).astype(BF16)
        return inverse - dot(shift, own[0]), jnp.sum(rest * rest)

    inverse, _ = polish(inverse)
    inverse, gap = polish(inverse)
    out_ref[...] = inverse

    def again(state):
        inverse, gap = polish(out_ref[...])
        out_ref[...] = inverse
        return state[0] + 1, gap

    _, gap = lax.while_loop(lambda state: (state[0] < 16) & (state[1] > SETTLED), again, (0, gap))
    settled = gap <= SETTLED

    @pl.when(settled)
    def _():
        out_ref[...] = out_ref[...] * scale_row

    @pl.when(jnp.logical_not(settled))
    def _():
        eliminate(block, out_ref, work_ref)


def bounds_of(count):
    return (0, -(-4 * count // 9), -(-7 * count // 9), count)


def tiles_of(low, high):
    return [(i, k) for k in range(high) for i in range(max(k, low), high)]


def gram_kernel(layout, bounds, parts, spot_ref, *refs):
    piece_refs, gram_refs = refs[: len(layout)], refs[len(layout) : len(layout) + len(bounds) - 1]
    mine_ref, sketch_ref, high_ref, low_ref, own_high_ref, own_low_ref, sems = refs[len(layout) + len(bounds) - 1 :]
    spot = spot_ref[0]
    sets, size, width = sketch_ref.shape
    step, part, rows = size // parts, TILE // parts, width // parts
    copies = []
    for n, (s, d, offset) in enumerate(layout):
        at = pl.multiple_of((spot ^ d) * step + offset, 8)
        target = sketch_ref.at[s, pl.ds(at, piece_refs[n].shape[0]), :]
        copies.append(pltpu.make_async_copy(piece_refs[n], target, sems.at[n]))
    for copy in copies:
        copy.start()
    for copy in copies:
        copy.wait()
    for s in range(sets):
        for i in range(bounds[-1]):
            here = slice(i * TILE, (i + 1) * TILE)
            values = sketch_ref[s, here, :]
            high_ref[s, here, :], low_ref[s, here, :] = halves(values)
            mine = values[:, :rows]
            for other in range(1, parts):
                mine = jnp.where(spot == other, values[:, other * rows : (other + 1) * rows], mine)
            mine_ref[s * rows : (s + 1) * rows, here] = mine.T
        for i in range(bounds[-1]):
            at = pl.multiple_of(i * TILE + spot * part, 16)
            own_high_ref[s, i * part : (i + 1) * part, :] = high_ref[s, pl.ds(at, part), :]
            own_low_ref[s, i * part : (i + 1) * part, :] = low_ref[s, pl.ds(at, part), :]
    for gram_ref, low, high in zip(gram_refs, bounds, bounds[1:]):
        done = 0
        for k in range(high):
            here, own = slice(k * TILE, (k + 1) * TILE), slice(max(k, low) * part, high * part)
            products = [
                dot3((own_high_ref[s, own, :], own_low_ref[s, own, :]), (high_ref[s, here, :], low_ref[s, here, :]), NT)
                for s in range(sets)
            ]
            gram_ref[done : done + own.stop - own.start, :] = sum(products)
            done += own.stop - own.start
        if done < gram_ref.shape[0]:
            gram_ref[done:, :] = jnp.zeros((gram_ref.shape[0] - done, TILE), F32)


def gram_shares(spot, sets, parts):
    layout = [(s, d, offset) for s, pieces in enumerate(sets) for d, offset, _ in pieces]
    arrays = [array for pieces in sets for _, _, array in pieces]
    width, rows = arrays[0].shape
    size = parts * width
    count, part = size // TILE, TILE // parts
    bounds = bounds_of(count)
    shapes = []
    for low, high in zip(bounds, bounds[1:]):
        tiles = len(tiles_of(low, high))
        shapes.append(jax.ShapeDtypeStruct(((tiles + tiles % 2) * part, TILE), F32))
    shapes.append(jax.ShapeDtypeStruct((len(sets) * rows // parts, size), F32))
    return pl.pallas_call(
        functools.partial(gram_kernel, layout, bounds, parts),
        out_shape=shapes,
        in_specs=[SMEM] + [ANY] * len(arrays),
        out_specs=[VMEM] * len(shapes),
        scratch_shapes=[
            pltpu.VMEM((len(sets), size, rows), F32),
            pltpu.VMEM((len(sets), size, rows), BF16),
            pltpu.VMEM((len(sets), size, rows), BF16),
            pltpu.VMEM((len(sets), count * part, rows), BF16),
            pltpu.VMEM((len(sets), count * part, rows), BF16),
            pltpu.SemaphoreType.DMA((len(arrays),)),
        ],
        compiler_params=pltpu.CompilerParams(vmem_limit_bytes=60 << 20),
        cost_estimate=pl.CostEstimate(
            flops=3 * size * size * rows // parts, bytes_accessed=8 * size * rows, transcendentals=0
        ),
    )(spot, *arrays)


def basis_kernel(scale, layout, cuts, parts, spot_ref, *refs):
    refs = list(refs)
    take = lambda n: [refs.pop(0) for _ in range(n)]
    share_refs = take(len(layout))
    (sketch_ref,) = take(1)
    past = [take(6) for _ in cuts[:-2]]
    basis_ref, short_ref, rest_ref, high_ref, low_ref, inv_high_ref, inv_low_ref = take(7)
    gram_ref, inverse_ref, work_ref, sems = refs
    first, last = cuts[-2:]
    part, half = TILE // parts, gram_ref.shape[2]
    spot, core = spot_ref[0], spot_ref[1]
    copies = []
    for n, (e, d, offset) in enumerate(layout):
        target = gram_ref.at[core ^ e, spot ^ d, pl.ds(offset, share_refs[n].shape[0]), :]
        copies.append(pltpu.make_async_copy(share_refs[n], target, sems.at[n]))
    for copy in copies:
        copy.start()
    for copy in copies:
        copy.wait()
    index = {tile: n * part for n, tile in enumerate(tiles_of(first, last))}

    def gram_rows(low, high, k):
        blocks = []
        for i in range(low, high):
            owner, at = divmod(index[i, k], half)
            blocks += [gram_ref[owner, sub, at : at + part, :] for sub in range(parts)]
        return scale * jnp.concatenate(blocks, axis=0)

    def rows_of(low, high, width):
        here = slice((low - first) * TILE, (high - first) * TILE)
        return high_ref[here, : width * TILE], low_ref[here, : width * TILE]

    def store_rows(low, high, k, values):
        here, cols = slice((low - first) * TILE, (high - first) * TILE), slice(k * TILE, (k + 1) * TILE)
        high_ref[here, cols], low_ref[here, cols] = halves(values)

    for (top, bottom), (_, _, past_high, past_low, past_inv_high, past_inv_low) in zip(zip(cuts, cuts[1:]), past):
        for k in range(top, bottom):
            here = slice((k - top) * TILE, (k - top + 1) * TILE)
            values = gram_rows(first, last, k)
            if k:
                factor = past_high[here, : k * TILE], past_low[here, : k * TILE]
                values = values - dot3(rows_of(first, last, k), factor, NT)
            own = past_inv_high[here, :], past_inv_low[here, :]
            store_rows(first, last, k, dot3(halves(values), own, NT))

    for k in range(first, last):
        here = slice((k - first) * TILE, (k - first + 1) * TILE)
        factor = rows_of(k, k + 1, k)

        def left_over(low, high):
            values = gram_rows(low, high, k)
            return values - dot3(rows_of(low, high, k), factor, NT) if k else values

        inverse_factor(left_over(k, k + 1), inverse_ref, work_ref)
        inv_high_ref[here, :], inv_low_ref[here, :] = halves(inverse_ref[...])
        own = inv_high_ref[here, :], inv_low_ref[here, :]
        if k + 1 < last:
            store_rows(k + 1, last, k, dot3(halves(left_over(k + 1, last)), own, NT))
        values = sketch_ref[:, here]
        for (top, bottom), (past_short, past_rest, *_) in zip(zip(cuts, cuts[1:]), past):
            cols = slice(top * TILE, bottom * TILE)
            values = values - dot3(
                (past_short[...], past_rest[...]), (factor[0][:, cols], factor[1][:, cols]), NT
            )
        if k > first:
            cols = slice(first * TILE, k * TILE)
            done = slice(0, (k - first) * TILE)
            values = values - dot3(
                (short_ref[:, done], rest_ref[:, done]), (factor[0][:, cols], factor[1][:, cols]), NT
            )
        solved = dot3(halves(values), own, NT)
        basis_ref[:, here] = solved
        short_ref[:, here], rest_ref[:, here] = halves(solved)


def basis_part(spots, shares, sketch, past, cuts, parts, scale):
    first, last = cuts[-2:]
    rows, width = sketch.shape
    layout = [(e, d, offset) for e, d, offset, _ in shares]
    arrays = [array for _, _, _, array in shares]
    half = (len(tiles_of(first, last)) + 1) // 2 * (TILE // parts)
    flat = [array for arrays_of_part in past for array in arrays_of_part]
    shape = jax.ShapeDtypeStruct
    size = last * TILE
    basis, *kept = pl.pallas_call(
        functools.partial(basis_kernel, scale, layout, cuts, parts),
        out_shape=[shape((rows, width), F32)]
        + [shape((rows, width), BF16)] * 2
        + [shape((width, size), BF16)] * 2
        + [shape((width, TILE), BF16)] * 2,
        in_specs=[SMEM] + [ANY] * len(arrays) + [VMEM] * (1 + len(flat)),
        out_specs=[VMEM] * 7,
        scratch_shapes=[
            pltpu.VMEM((2, parts, half, TILE), F32),
            pltpu.VMEM((TILE, TILE), F32),
            pltpu.VMEM((TILE, TILE), F32),
            pltpu.SemaphoreType.DMA((len(arrays),)),
        ],
        compiler_params=pltpu.CompilerParams(vmem_limit_bytes=60 << 20),
        cost_estimate=pl.CostEstimate(
            flops=128 * size * size * width, bytes_accessed=4 * size * width, transcendentals=0
        ),
    )(spots, *arrays, sketch, *flat)
    return basis, kept


def swapped(x, axis, distance):
    return lax.ppermute(x, axis, [(i, i ^ distance) for i in range(lax.axis_size(axis))])


def together(*arrays):
    return lax.optimization_barrier(arrays)


def row_pieces(x, direct=False):
    size = lax.axis_size("row")
    if size != 4 or direct:
        return [(0, 0, x)] + [(d, 0, swapped(x, "row", d)) for d in range(1, size)]
    half = x.shape[0] // 2
    first, second = x[:half], x[half:]
    first_one, second_two, first_two, second_one = together(
        swapped(first, "row", 1), swapped(second, "row", 2), swapped(first, "row", 2), swapped(second, "row", 1)
    )
    first_three, second_three = swapped(first_one, "row", 2), swapped(second_two, "row", 1)
    return [
        (0, 0, x),
        (1, 0, first_one),
        (1, half, second_one),
        (2, 0, first_two),
        (2, half, second_two),
        (3, 0, first_three),
        (3, half, second_three),
    ]


def in_row_order(pieces, place):
    step, cols = pieces[0][2].shape
    size = lax.axis_size("row")
    whole = jnp.zeros((step * size, cols), pieces[0][2].dtype)
    for d in range(size):
        block = jnp.concatenate([piece for e, _, piece in pieces if e == d], axis=0)
        whole = lax.dynamic_update_slice_in_dim(whole, block, (place ^ d) * step, 0)
    return whole


def gathered_chips(x):
    spread = jnp.broadcast_to(x[None], (lax.axis_size("chip"),) + x.shape)
    return lax.all_to_all(spread, "chip", 0, 0).reshape(-1, x.shape[1])


def on_device(left_site, right_site, gate, omega):
    parts, chips = lax.axis_size("row"), lax.axis_size("chip")
    total_rows = left_site.shape[0] * parts
    place, chip, core = lax.axis_index("row"), lax.axis_index("chip"), lax.axis_index("core")
    spots = jnp.stack([place, core, chip]).astype(jnp.int32)
    left_sets = left_site.reshape(chips * lax.axis_size("core"), 2, -1, left_site.shape[1])
    right_cols = in_row_order(row_pieces(right_site), place)

    thetas, sets = [], []
    for s in range(2):
        left = left_sets[:, s].reshape(-1, left_site.shape[1])
        pieces = [left] + [swapped(left, "chip", d) for d in range(1, chips)]
        thetas.append(pieces)
    for s in range(2):
        pieces = thetas[s] + [swapped(x, "core", 1) for x in thetas[s]]
        theta = theta_of(gate, spots, pieces, right_cols)
        if s == 0:
            theta, *thetas[1] = together(theta, *thetas[1])
        thetas[s] = theta.reshape(left_sets.shape[0], -1, theta.shape[1])
        theta_set = in_row_order(row_pieces(lax.all_to_all(theta, COL, 0, 1, tiled=True)), place)
        sets.append(row_pieces(dot(omega, theta_set, (((0,), (1,)), ((), ())))))
    theta = jnp.stack(thetas, axis=1).reshape(-1, right_cols.shape[1])
    cols_here = theta.shape[1]
    *gram, sketch = gram_shares(spots, sets, parts)
    bounds = bounds_of(sketch.shape[1] // TILE)

    halved = []
    for share in gram:
        half = share.shape[0] // 2
        kept = lax.dynamic_slice_in_dim(share, core * half, half, 0)
        given = lax.dynamic_slice_in_dim(share, (1 - core) * half, half, 0)
        halved.append((kept + swapped(given, "core", 1)).reshape(chips, half // chips, TILE))
    lengths = [x.shape[1] for x in halved]
    summed = jnp.sum(lax.all_to_all(jnp.concatenate(halved, axis=1), "chip", 0, 0), axis=0)
    gathered = []
    for n, length in enumerate(lengths):
        share = summed[sum(lengths[:n]) : sum(lengths[: n + 1])]
        gathered.append(gathered_chips(share))

    past, basis, rows, mine = [], [], [], []
    for n in range(len(gathered)):
        mine.append(row_pieces(gathered[n], direct=True))
        if n:
            arrays = together(past[-1][0], *[x for _, _, x in mine[n]])
            past[-1][0] = arrays[0]
            mine[n] = [(d, at, x) for (d, at, _), x in zip(mine[n], arrays[1:])]
        shares = [(0, d, at, x) for d, at, x in mine[n]]
        shares += [(1, d, at, swapped(x, "core", 1)) for d, at, x in mine[n]]
        cuts = bounds[: n + 2]
        columns = sketch[:, cuts[-2] * TILE : cuts[-1] * TILE]
        if n == 0:
            columns, gathered[1] = together(columns, gathered[1])
        if n > 1:
            columns, rows[n - 2] = together(columns, rows[n - 2])
        done, kept = basis_part(spots, shares, columns, past, cuts, parts, 1.0 / total_rows)
        past.append(kept)
        basis.append(done)
        short = kept[0]
        if n:
            short, rows[n - 1] = together(short, rows[n - 1])
        rows.append(lax.all_gather(short, COL, axis=0, tiled=True))

    folded = [dot(part, theta, TN).astype(BF16) for part in rows]
    folded = jnp.concatenate(folded, axis=0).reshape(parts, -1, cols_here)
    sums = lax.all_to_all(folded, "row", 0, 0)
    projected = jnp.sum(sums.astype(F32), axis=0) / math.sqrt(total_rows)
    return (jnp.concatenate(basis, axis=1), projected)


COL = ("chip", "core")


def solution(mesh):
    row, col = mesh.devices.shape
    split = Mesh(mesh.devices.reshape(row, col // 2, 2), ("row",) + COL)
    in_specs = (P("row", COL), P("row", COL), P(), P(None, "row"))
    out_specs = (P(("row",) + COL, None), P("row", COL))
    return jax.shard_map(
        on_device, mesh=split, in_specs=in_specs, out_specs=out_specs, check_vma=False
    )
```

```python
import functools
import math

import jax
import jax.numpy as jnp
from jax import lax
from jax.experimental import pallas as pl
from jax.experimental.pallas import tpu as pltpu
from jax.sharding import Mesh, PartitionSpec as P

F32, BF16 = jnp.float32, jnp.bfloat16
NN = (((1,), (0,)), ((), ()))
NT = (((1,), (1,)), ((), ()))
TN = (((0,), (0,)), ((), ()))
VMEM = pl.BlockSpec(memory_space=pltpu.VMEM)
SMEM = pl.BlockSpec(memory_space=pltpu.SMEM)
ANY = pl.BlockSpec(memory_space=pl.ANY)
TILE = 256
ROUGH_STEPS = 5
SETTLED = 1e-4


def dot(a, b, dims=NN):
    return lax.dot_general(a, b, dims, preferred_element_type=F32)


def halves(x):
    high = x.astype(BF16)
    return high, (x - high.astype(F32)).astype(BF16)


def dot3(a, b, dims=NN):
    return dot(a[0], b[0], dims) + dot(a[0], b[1], dims) + dot(a[1], b[0], dims)


def positions(shape):
    return lax.broadcasted_iota(jnp.int32, shape, 0), lax.broadcasted_iota(jnp.int32, shape, 1)


def theta_kernel(chips, gate_ref, spot_ref, *refs):
    left_refs, right_ref, theta_ref = refs[:-2], refs[-2], refs[-1]
    depth = left_refs[0].shape[1]
    bare = None
    for n, left_ref in enumerate(left_refs):
        e, d = divmod(n, chips)
        at = ((spot_ref[2] ^ d) * 2 + (spot_ref[1] ^ e)) * depth
        product = dot(left_ref[...], right_ref[pl.ds(pl.multiple_of(at, depth), depth), :])
        bare = product if bare is None else bare + product
    rows, cols = bare.shape
    row, col = positions((rows, cols))
    row_odd, col_odd = row % 2 == 1, col % 2 == 1

    def partner_row(x):
        return jnp.where(row_odd, pltpu.roll(x, 1, 0), pltpu.roll(x, rows - 1, 0))

    def partner_col(x):
        return jnp.where(col_odd, pltpu.roll(x, 1, 1), pltpu.roll(x, cols - 1, 1))

    def weight(flip_row, flip_col):
        def entry(s, t):
            return gate_ref[2 * s + t, 2 * (s ^ flip_row) + (t ^ flip_col)]

        return jnp.where(
            row_odd,
            jnp.where(col_odd, entry(1, 1), entry(1, 0)),
            jnp.where(col_odd, entry(0, 1), entry(0, 0)),
        )

    across = partner_row(bare)
    mixed = weight(0, 0) * bare + weight(0, 1) * partner_col(bare)
    mixed = mixed + weight(1, 0) * across + weight(1, 1) * partner_col(across)
    theta_ref[...] = mixed.astype(BF16)


def theta_of(gate, spots, pieces, right):
    rows, depth = pieces[0].shape
    cols = right.shape[1]
    tile = min(TILE, rows)
    return pl.pallas_call(
        functools.partial(theta_kernel, len(pieces) // 2),
        grid=(rows // tile,),
        out_shape=jax.ShapeDtypeStruct((rows, cols), BF16),
        in_specs=[SMEM, SMEM]
        + [pl.BlockSpec((tile, depth), lambda i: (i, 0))] * len(pieces)
        + [pl.BlockSpec(right.shape, lambda i: (0, 0))],
        out_specs=pl.BlockSpec((tile, cols), lambda i: (i, 0)),
        compiler_params=pltpu.CompilerParams(vmem_limit_bytes=32 << 20),
        cost_estimate=pl.CostEstimate(
            flops=rows * cols,
            bytes_accessed=rows * cols,
            transcendentals=0,
        ),
    )(gate, spots, *pieces, right)


def eliminate(block, out_ref, work_ref):
    tile = block.shape[0]
    row, col = positions((tile, tile))
    work_ref[...] = block
    out_ref[...] = jnp.where(row == col, 1.0, 0.0).astype(F32)

    def column(j, carry):
        values = work_ref[...]
        pivot_row = work_ref[pl.ds(j, 1), :]
        pivot_col = jnp.sum(jnp.where(col == j, values, 0.0), axis=1, keepdims=True)
        pivot = jnp.sum(jnp.where(col[:1] == j, pivot_row, 0.0), axis=1, keepdims=True)
        root = 1.0 / jnp.sqrt(pivot)
        done = out_ref[pl.ds(j, 1), :] * root
        factor = jnp.where(row[:, :1] > j, pivot_col * root, 0.0)
        work_ref[...] = values - factor * (pivot_row * root)
        out_ref[...] = out_ref[...] - factor * done
        out_ref[pl.ds(j, 1), :] = done
        return carry

    lax.fori_loop(0, tile, column, 0)


def inverse_factor(block, out_ref, work_ref):
    row, col = positions(block.shape)
    same, below = row == col, row > col
    diagonal = jnp.where(same, block, 0.0)
    scale_row = lax.rsqrt(jnp.sum(diagonal, axis=0, keepdims=True))
    scale_col = lax.rsqrt(jnp.sum(diagonal, axis=1, keepdims=True))
    normal = block * scale_row * scale_col
    parts = halves(normal)
    near = 0.5 * normal
    inverse = jnp.where(same, math.sqrt(0.5), 0.0).astype(F32)
    for _ in range(ROUGH_STEPS):
        step = jnp.where(below, -near, jnp.where(same, 1.5 - 0.5 * near, 0.0)).astype(BF16)
        inverse = dot(step, inverse.astype(BF16))
        near = dot(dot(step, near.astype(BF16)).astype(BF16), step, NT)

    def polish(inverse):
        own = halves(inverse)
        rest = dot3(halves(dot3(own, parts)), own, NT) - jnp.where(same, 1.0, 0.0)
        shift = jnp.where(below, rest, jnp.where(same, 0.5 * rest, 0.0)).astype(BF16)
        return inverse - dot(shift, own[0]), jnp.sum(rest * rest)

    inverse, _ = polish(inverse)
    inverse, gap = polish(inverse)
    out_ref[...] = inverse

    def again(state):
        inverse, gap = polish(out_ref[...])
        out_ref[...] = inverse
        return state[0] + 1, gap

    _, gap = lax.while_loop(lambda state: (state[0] < 16) & (state[1] > SETTLED), again, (0, gap))
    settled = gap <= SETTLED

    @pl.when(settled)
    def _():
        out_ref[...] = out_ref[...] * scale_row

    @pl.when(jnp.logical_not(settled))
    def _():
        eliminate(block, out_ref, work_ref)


def bounds_of(count):
    return (0, -(-4 * count // 9), -(-7 * count // 9), count)


def tiles_of(low, high):
    return [(i, k) for k in range(high) for i in range(max(k, low), high)]


def lengths_of(bounds, part):
    return [(len(tiles_of(low, high)) + 1) // 2 * part for low, high in zip(bounds, bounds[1:])]


def gram_kernel(layout, bounds, parts, spot_ref, *refs):
    piece_refs, refs = refs[: len(layout)], refs[len(layout) :]
    kept_ref, given_ref, mine_ref, gram_ref, sketch_ref, high_ref, low_ref, own_high_ref, own_low_ref, sems = refs
    spot, core = spot_ref[0], spot_ref[1]
    sets, size, width = sketch_ref.shape
    step, part, rows = size // parts, TILE // parts, width // parts
    copies = []
    for n, (s, d, offset) in enumerate(layout):
        at = pl.multiple_of((spot ^ d) * step + offset, 8)
        target = sketch_ref.at[s, pl.ds(at, piece_refs[n].shape[0]), :]
        copies.append(pltpu.make_async_copy(piece_refs[n], target, sems.at[n]))
    for copy in copies:
        copy.start()
    for copy in copies:
        copy.wait()
    for s in range(sets):
        for i in range(bounds[-1]):
            here = slice(i * TILE, (i + 1) * TILE)
            values = sketch_ref[s, here, :]
            high_ref[s, here, :], low_ref[s, here, :] = halves(values)
        for i in range(bounds[-1]):
            at = pl.multiple_of(i * TILE + spot * part, 16)
            own_high_ref[s, i * part : (i + 1) * part, :] = high_ref[s, pl.ds(at, part), :]
            own_low_ref[s, i * part : (i + 1) * part, :] = low_ref[s, pl.ds(at, part), :]
    lengths = lengths_of(bounds, part)
    chips = gram_ref.shape[1]
    base = 0
    for length, low, high in zip(lengths, bounds, bounds[1:]):
        step, at = length // chips, 0

        def store(at, values):
            done = 0
            while done < values.shape[0]:
                owner, rest = divmod(at + done, length)
                chip, offset = divmod(rest, step)
                rows = min(values.shape[0] - done, step - offset)
                gram_ref[owner, chip, base + offset : base + offset + rows, :] = values[done : done + rows]
                done += rows
            return at + done

        for k in range(high):
            here, own = slice(k * TILE, (k + 1) * TILE), slice(max(k, low) * part, high * part)
            products = [
                dot3((own_high_ref[s, own, :], own_low_ref[s, own, :]), (high_ref[s, here, :], low_ref[s, here, :]), NT)
                for s in range(sets)
            ]
            at = store(at, sum(products))
        if at < 2 * length:
            store(at, jnp.zeros((2 * length - at, TILE), F32))
        base += step
    copies = [
        pltpu.make_async_copy(gram_ref.at[core], kept_ref, sems.at[0]),
        pltpu.make_async_copy(gram_ref.at[1 - core], given_ref, sems.at[1]),
    ]
    for copy in copies:
        copy.start()
    for s in range(sets):
        for i in range(bounds[-1]):
            here = slice(i * TILE, (i + 1) * TILE)
            values = sketch_ref[s, here, :]
            mine = values[:, :rows]
            for other in range(1, parts):
                mine = jnp.where(spot == other, values[:, other * rows : (other + 1) * rows], mine)
            mine_ref[s * rows : (s + 1) * rows, here] = mine.T
    for copy in copies:
        copy.wait()


def gram_shares(spots, sets, parts, chips):
    layout = [(s, d, offset) for s, pieces in enumerate(sets) for d, offset, _ in pieces]
    arrays = [array for pieces in sets for _, _, array in pieces]
    width, rows = arrays[0].shape
    size = parts * width
    count, part = size // TILE, TILE // parts
    bounds = bounds_of(count)
    shared = (chips, sum(lengths_of(bounds, part)) // chips, TILE)
    shape = jax.ShapeDtypeStruct
    return pl.pallas_call(
        functools.partial(gram_kernel, layout, bounds, parts),
        out_shape=[shape(shared, F32), shape(shared, F32), shape((len(sets) * rows // parts, size), F32)],
        in_specs=[SMEM] + [ANY] * len(arrays),
        out_specs=[ANY, ANY, VMEM],
        scratch_shapes=[
            pltpu.VMEM((2,) + shared, F32),
            pltpu.VMEM((len(sets), size, rows), F32),
            pltpu.VMEM((len(sets), size, rows), BF16),
            pltpu.VMEM((len(sets), size, rows), BF16),
            pltpu.VMEM((len(sets), count * part, rows), BF16),
            pltpu.VMEM((len(sets), count * part, rows), BF16),
            pltpu.SemaphoreType.DMA((len(arrays),)),
        ],
        compiler_params=pltpu.CompilerParams(vmem_limit_bytes=60 << 20),
        cost_estimate=pl.CostEstimate(
            flops=3 * size * size * rows // parts, bytes_accessed=8 * size * rows, transcendentals=0
        ),
    )(spots, *arrays)


def basis_kernel(scale, layout, cuts, parts, final, spot_ref, *refs):
    refs = list(refs)

    def take(number):
        return [refs.pop(0) for _ in range(number)]

    share_refs = take(len(layout))
    (sketch_ref,) = take(1)
    past_refs = [take(6) for _ in cuts[:-2]]
    first, last = cuts[-2:]
    if final:
        basis_ref, short_ref, rest_ref, inv_high_ref, inv_low_ref = take(5)
    else:
        basis_ref, short_ref, rest_ref, high_out, low_out, inv_high_ref, inv_low_ref = take(7)
    high_ref, low_ref, gram_ref, inverse_ref, work_ref = take(5)
    past = [take(6) for _ in cuts[:-2]]
    sems, past_sems, out_sems = refs
    part, half = TILE // parts, gram_ref.shape[2]
    spot, core = spot_ref[0], spot_ref[1]
    copies = []
    for n, (e, d, offset) in enumerate(layout):
        target = gram_ref.at[core ^ e, spot ^ d, pl.ds(offset, share_refs[n].shape[0]), :]
        copies.append(pltpu.make_async_copy(share_refs[n], target, sems.at[n]))
    for copy in copies:
        copy.start()
    whole_copies, row_copies = [], []
    for n, (sources, targets, top, bottom) in enumerate(zip(past_refs, past, cuts, cuts[1:])):
        whole_copies.append(
            [pltpu.make_async_copy(sources[m], targets[m], past_sems.at[n, m]) for m in (0, 1, 4, 5)]
        )
        for k in range(top, bottom):
            here, cols = pl.ds((k - top) * TILE, TILE), pl.ds(0, k * TILE)
            row_copies.append(
                [
                    pltpu.make_async_copy(
                        sources[m].at[here, cols], targets[m].at[here, cols], past_sems.at[n, 4 + m + 2 * (k - top)]
                    )
                    for m in (2, 3)
                    if k
                ]
            )
    for group in whole_copies:
        group[2].start()
        group[3].start()
    for group in row_copies:
        for copy in group:
            copy.start()
    for group in whole_copies:
        group[0].start()
        group[1].start()
    out_copies = []

    def send(k, start):
        if not final and start < (last - first) * TILE:
            here, cols = pl.ds(start, (last - first) * TILE - start), pl.ds(k * TILE, TILE)
            for m, (source, target) in enumerate(((high_ref, high_out), (low_ref, low_out))):
                copy = pltpu.make_async_copy(source.at[here, cols], target.at[here, cols], out_sems.at[m, k])
                copy.start()
                out_copies.append(copy)

    for copy in copies:
        copy.wait()
    index = {tile: n * part for n, tile in enumerate(tiles_of(first, last))}

    def gram_rows(low, high, k):
        blocks = []
        for i in range(low, high):
            owner, at = divmod(index[i, k], half)
            blocks += [gram_ref[owner, sub, at : at + part, :] for sub in range(parts)]
        return scale * jnp.concatenate(blocks, axis=0)

    def rows_of(low, high, width):
        here = slice((low - first) * TILE, (high - first) * TILE)
        return high_ref[here, : width * TILE], low_ref[here, : width * TILE]

    def store_rows(low, high, k, values):
        here, cols = slice((low - first) * TILE, (high - first) * TILE), slice(k * TILE, (k + 1) * TILE)
        high_ref[here, cols], low_ref[here, cols] = halves(values)

    for n, (top, bottom) in enumerate(zip(cuts[:-2], cuts[1:])):
        _, _, past_high, past_low, past_inv_high, past_inv_low = past[n]
        for k in range(top, bottom):
            if k == top:
                whole_copies[n][2].wait()
                whole_copies[n][3].wait()
            for copy in row_copies[k]:
                copy.wait()
            here = slice((k - top) * TILE, (k - top + 1) * TILE)
            values = gram_rows(first, last, k)
            if k:
                factor = past_high[here, : k * TILE], past_low[here, : k * TILE]
                values = values - dot3(rows_of(first, last, k), factor, NT)
            own = past_inv_high[here, :], past_inv_low[here, :]
            store_rows(first, last, k, dot3(halves(values), own))
            send(k, 0)

    for group in whole_copies:
        group[0].wait()
        group[1].wait()
    for k in range(first, last):
        here = slice((k - first) * TILE, (k - first + 1) * TILE)
        factor = rows_of(k, k + 1, k)

        def left_over(low, high):
            values = gram_rows(low, high, k)
            return values - dot3(rows_of(low, high, k), factor, NT) if k else values

        inverse_factor(left_over(k, k + 1), inverse_ref, work_ref)
        inv_high_ref[here, :], inv_low_ref[here, :] = halves(inverse_ref[...].T)
        own = inv_high_ref[here, :], inv_low_ref[here, :]
        if k + 1 < last:
            store_rows(k + 1, last, k, dot3(halves(left_over(k + 1, last)), own))
            send(k, (k + 1 - first) * TILE)
        values = sketch_ref[:, here]
        for (top, bottom), (past_short, past_rest, *_) in zip(zip(cuts, cuts[1:]), past):
            cols = slice(top * TILE, bottom * TILE)
            values = values - dot3(
                (past_short[...], past_rest[...]), (factor[0][:, cols], factor[1][:, cols]), NT
            )
        if k > first:
            cols = slice(first * TILE, k * TILE)
            done = slice(0, (k - first) * TILE)
            values = values - dot3(
                (short_ref[:, done], rest_ref[:, done]), (factor[0][:, cols], factor[1][:, cols]), NT
            )
        solved = dot3(halves(values), own)
        basis_ref[:, here] = solved
        short_ref[:, here], rest_ref[:, here] = halves(solved)
    for copy in out_copies:
        copy.wait()


def basis_part(spots, shares, sketch, past, cuts, parts, scale, final):
    first, last = cuts[-2:]
    rows, width = sketch.shape
    layout = [(e, d, offset) for e, d, offset, _ in shares]
    arrays = [array for _, _, _, array in shares]
    half = (len(tiles_of(first, last)) + 1) // 2 * (TILE // parts)
    flat = [array for arrays_of_part in past for array in arrays_of_part]
    shape = jax.ShapeDtypeStruct
    size = last * TILE
    factor = shape((width, size), BF16)
    kept_shapes = [shape((rows, width), BF16)] * 2 + [factor] * 2 + [shape((width, TILE), BF16)] * 2
    kept_specs = [VMEM, VMEM, ANY, ANY, VMEM, VMEM]
    scratch = [pltpu.VMEM((width, size), BF16)] * 2
    scratch += [pltpu.VMEM((2, parts, half, TILE), F32)] + [pltpu.VMEM((TILE, TILE), F32)] * 2
    scratch += [pltpu.VMEM(x.shape, x.dtype) for x in flat]
    scratch += [
        pltpu.SemaphoreType.DMA((len(arrays),)),
        pltpu.SemaphoreType.DMA((max(len(past), 1), 6 + 2 * last)),
        pltpu.SemaphoreType.DMA((2, last)),
    ]
    if final:
        scratch = [pltpu.VMEM(kept_shapes[n].shape, BF16) for n in (1, 4, 5)] + scratch
        kept_shapes, kept_specs = kept_shapes[:1], kept_specs[:1]
    basis, *kept = pl.pallas_call(
        functools.partial(basis_kernel, scale, layout, cuts, parts, final),
        out_shape=[shape((rows, width), F32)] + kept_shapes,
        in_specs=[SMEM] + [ANY] * len(arrays) + [VMEM] + [ANY] * len(flat),
        out_specs=[VMEM] + kept_specs,
        scratch_shapes=scratch,
        compiler_params=pltpu.CompilerParams(vmem_limit_bytes=60 << 20),
        cost_estimate=pl.CostEstimate(
            flops=128 * size * size * width, bytes_accessed=4 * size * width, transcendentals=0
        ),
    )(spots, *arrays, sketch, *flat)
    return basis, kept


def swapped(x, axis, distance):
    return lax.ppermute(x, axis, [(i, i ^ distance) for i in range(lax.axis_size(axis))])


def together(*arrays):
    return lax.optimization_barrier(arrays)


def row_pieces(x, direct=False):
    size = lax.axis_size("row")
    if size != 4 or direct:
        return [(0, 0, x)] + [(d, 0, swapped(x, "row", d)) for d in range(1, size)]
    half = x.shape[0] // 2
    first, second = x[:half], x[half:]
    first_one, second_two, first_two, second_one = together(
        swapped(first, "row", 1), swapped(second, "row", 2), swapped(first, "row", 2), swapped(second, "row", 1)
    )
    first_three, second_three = swapped(first_one, "row", 2), swapped(second_two, "row", 1)
    return [
        (0, 0, x),
        (1, 0, first_one),
        (1, half, second_one),
        (2, 0, first_two),
        (2, half, second_two),
        (3, 0, first_three),
        (3, half, second_three),
    ]


def in_row_order(pieces, place):
    step, cols = pieces[0][2].shape
    size = lax.axis_size("row")
    whole = jnp.zeros((step * size, cols), pieces[0][2].dtype)
    for d in range(size):
        block = jnp.concatenate([piece for e, _, piece in pieces if e == d], axis=0)
        whole = lax.dynamic_update_slice_in_dim(whole, block, (place ^ d) * step, 0)
    return whole


def gathered_chips(x):
    spread = jnp.broadcast_to(x[None], (lax.axis_size("chip"),) + x.shape)
    return lax.all_to_all(spread, "chip", 0, 0).reshape(-1, x.shape[1])


def on_device(left_site, right_site, gate, omega):
    parts, chips = lax.axis_size("row"), lax.axis_size("chip")
    total_rows = left_site.shape[0] * parts
    place, chip, core = lax.axis_index("row"), lax.axis_index("chip"), lax.axis_index("core")
    spots = jnp.stack([place, core, chip]).astype(jnp.int32)
    left_sets = left_site.reshape(chips * lax.axis_size("core"), 2, -1, left_site.shape[1])
    right_cols = in_row_order(row_pieces(right_site), place)

    thetas, sets = [], []
    for s in range(2):
        left = left_sets[:, s].reshape(-1, left_site.shape[1])
        pieces = [left] + [swapped(left, "chip", d) for d in range(1, chips)]
        thetas.append(pieces)
    for s in range(2):
        pieces = thetas[s] + [swapped(x, "core", 1) for x in thetas[s]]
        theta = theta_of(gate, spots, pieces, right_cols)
        if s == 0:
            theta, *thetas[1] = together(theta, *thetas[1])
        thetas[s] = theta.reshape(left_sets.shape[0], -1, theta.shape[1])
        theta_set = in_row_order(row_pieces(lax.all_to_all(theta, COL, 0, 1, tiled=True)), place)
        sets.append(row_pieces(dot(omega, theta_set, (((0,), (1,)), ((), ())))))
    theta = jnp.stack(thetas, axis=1).reshape(-1, right_cols.shape[1])
    cols_here = theta.shape[1]
    kept, given, sketch = gram_shares(spots, sets, parts, chips)
    bounds = bounds_of(sketch.shape[1] // TILE)
    lengths = [length // chips for length in lengths_of(bounds, TILE // parts)]
    summed = jnp.sum(lax.all_to_all(kept + swapped(given, "core", 1), "chip", 0, 0), axis=0)
    gathered = []
    for n, length in enumerate(lengths):
        share = summed[sum(lengths[:n]) : sum(lengths[: n + 1])]
        gathered.append(gathered_chips(share))

    past, basis, rows, mine = [], [], [], []
    for n in range(len(gathered)):
        mine.append(row_pieces(gathered[n], direct=True))
        if n:
            arrays = together(past[-1][0], *[x for _, _, x in mine[n]])
            past[-1][0] = arrays[0]
            mine[n] = [(d, at, x) for (d, at, _), x in zip(mine[n], arrays[1:])]
        shares = [(0, d, at, x) for d, at, x in mine[n]]
        shares += [(1, d, at, swapped(x, "core", 1)) for d, at, x in mine[n]]
        cuts = bounds[: n + 2]
        columns = sketch[:, cuts[-2] * TILE : cuts[-1] * TILE]
        if n == 0:
            columns, gathered[1] = together(columns, gathered[1])
        if n > 1:
            columns, rows[n - 2] = together(columns, rows[n - 2])
        done, kept = basis_part(spots, shares, columns, past, cuts, parts, 1.0 / total_rows, n + 2 == len(bounds))
        past.append(kept)
        basis.append(done)
        short = kept[0]
        if n:
            short, rows[n - 1] = together(short, rows[n - 1])
        rows.append(lax.all_gather(short, COL, axis=0, tiled=True))

    folded = [dot(part, theta, TN).astype(BF16) for part in rows]
    folded = jnp.concatenate(folded, axis=0).reshape(parts, -1, cols_here)
    sums = lax.all_to_all(folded, "row", 0, 0)
    projected = jnp.sum(sums.astype(F32), axis=0) / math.sqrt(total_rows)
    return (jnp.concatenate(basis, axis=1), projected)


COL = ("chip", "core")


def solution(mesh):
    row, col = mesh.devices.shape
    split = Mesh(mesh.devices.reshape(row, col // 2, 2), ("row",) + COL)
    in_specs = (P("row", COL), P("row", COL), P(), P(None, "row"))
    out_specs = (P(("row",) + COL, None), P("row", COL))
    return jax.shard_map(
        on_device, mesh=split, in_specs=in_specs, out_specs=out_specs, check_vma=False
    )
```
